32 devices in a mesh: slab: 8 (over z, y), grp: 4 (over x, core).
Axes of the slice: x: 2, y: 2, z: 4, core: 2. Of those that a mesh axis runs over, the one named last changes fastest.
Arguments:
- positions: float32 [32, 16, 3, 128], P('slab', 'grp'), may hold values from 0 to 1
- sketch: bfloat16 [32, 16, 128, 256], P('slab', 'grp'), may hold values from -6 to 6
- counts: int32 [32, 16], P('slab', 'grp'), may hold values from 32 to 128, as said below
- neighbours: int32 [32, 16, 8], P('slab', 'grp'), may hold values from 0 to 8, as said below
Outputs:
- basis: bfloat16 [32, 16, 128, 256], P('slab', 'grp')
- factor: float32 [256, 256], replicated
The draws below stay inside these ranges and needn't reach their ends.
Inputs may be any that keep to these rules, and one draw needn't show every extreme that they name: `counts`: the first block of every device's region of 4 x 4 blocks is full. `neighbours`: a code is 3 (dz + 1) + (dy + 1) for offsets dz, dy in -1, 0, 1; the codes of one block are distinct and always include 4 (the block itself); each block leaves out exactly one of its nine codes, and the lists are symmetric: block a lists block b if and only if block b lists block a; the left-out pairs lie inside aligned 2 x 2 squares of blocks.
All inputs are finite; a program needn't handle non-finite values.
Results may differ from the reference program's by a relative error of at most 0.017.
Values may be sent and summed in bfloat16 or wider, within the bound.
A program may use at most 64 MiB of HBM per device.

```python
import math
import jax
import jax.numpy as jnp
from jax import lax

BLOCK_PTS = 128
SKETCH = 256
SLOTS = 8
BZ_DEV = 4
BY_DEV = 4
BZ = 32
BY = 16


def draw_counts(key, part):
    values = jax.random.randint(key, (BZ, BY), BLOCK_PTS // 4, BLOCK_PTS + 1)
    row_ids = lax.broadcasted_iota(jnp.int32, (BZ, BY), 0)
    col_ids = lax.broadcasted_iota(jnp.int32, (BZ, BY), 1)
    full_block = (row_ids % BZ_DEV == 0) & (col_ids % BY_DEV == 0)
    return jnp.where(full_block, BLOCK_PTS, values).astype(jnp.int32)


def draw_neighbours(key, part):
    pair_key = jax.random.fold_in(key, 11)
    order_key = jax.random.fold_in(key, 23)
    pairing = jax.random.randint(pair_key, (BZ // 2, BY // 2), 0, 3)
    pairing = jnp.repeat(jnp.repeat(pairing, 2, axis=0), 2, axis=1)
    row_par = lax.broadcasted_iota(jnp.int32, (BZ, BY), 0) % 2
    col_par = lax.broadcasted_iota(jnp.int32, (BZ, BY), 1) % 2
    flip_row = (pairing >= 1).astype(jnp.int32)
    flip_col = ((pairing == 0) | (pairing == 2)).astype(jnp.int32)
    shift_z = flip_row * (1 - 2 * row_par)
    shift_y = flip_col * (1 - 2 * col_par)
    dropped = 3 * (shift_z + 1) + (shift_y + 1)
    codes = jnp.arange(9, dtype=jnp.int32)
    scores = jax.random.randint(order_key, (BZ, BY, 9), 0, 2 ** 20) * 16 + codes
    scores = jnp.where(codes[None, None, :] == dropped[:, :, None], 2 ** 28, scores)
    order = jnp.argsort(scores, axis=-1)
    return order[..., :SLOTS].astype(jnp.int32)


def level_of(rng, extent, shards, smallest, top_value):
    loudness, own = 1.0, jax.random.fold_in(rng, 6)
    for position, shards_of in shards:
        draws = jnp.exp(jax.random.uniform(jax.random.fold_in(own, position), (shards_of,), jnp.float32, smallest / len(shards), top_value / len(shards)))
        loudness = loudness * jnp.repeat(draws, extent[position] // shards_of).reshape([-1 if axis == position else 1 for axis in range(len(extent))])
    return loudness


def scatter_about(key, dims, spread, limit, split=(), kind=jnp.bfloat16):
    entries = spread * jax.random.normal(key, dims, jnp.float32)
    if split:
        entries = entries * level_of(key, dims, split, -0.22, 0.18)
    return jnp.clip(entries, -limit, limit).astype(kind)


def setup_inputs(seed: int = 0) -> dict:
    streams_of = jax.random.split(jax.random.key(seed), 5)
    return {
        "positions": jnp.clip(1.0 * jax.random.uniform(streams_of[0], (BZ, BY, 3, BLOCK_PTS), jnp.float32) ** level_of(streams_of[0], (BZ, BY, 3, BLOCK_PTS), ((0, 8), (1, 4)), -0.2, 0.2), 0.0, 1.0),
        "sketch": scatter_about(streams_of[1], (BZ, BY, BLOCK_PTS, SKETCH), 1.0, 6.0, ((0, 8), (1, 4))),
        "counts": draw_counts(jax.random.fold_in(streams_of[4], 71), 0),
        "neighbours": draw_neighbours(jax.random.fold_in(streams_of[4], 71), 0),
    }


def kernel_tile(own_pos, other_pos, shift_z, shift_y):
    diff_z = other_pos[..., 0, None, :] + shift_z[..., None, None] - own_pos[..., 0, :, None]
    diff_y = other_pos[..., 1, None, :] + shift_y[..., None, None] - own_pos[..., 1, :, None]
    diff_x = other_pos[..., 2, None, :] - own_pos[..., 2, :, None]
    radius = jnp.sqrt(diff_z * diff_z + diff_y * diff_y + diff_x * diff_x)
    taper = jnp.maximum(1.0 - radius, 0.0)
    return taper ** 4 * (4.0 * radius + 1.0)

def reference(positions, sketch, counts, neighbours):
    blocks_z, blocks_y = counts.shape
    live_mask = jnp.arange(BLOCK_PTS, dtype=jnp.int32)[None, None, :] < counts[:, :, None]
    masked = jnp.where(live_mask[..., None], sketch, jnp.zeros_like(sketch))
    column_ids = jnp.arange(blocks_y, dtype=jnp.int32)

    def one_row(block_row):
        own_pos = positions[block_row]
        total = jnp.zeros((blocks_y, BLOCK_PTS, SKETCH), jnp.float32)
        for slot_index in range(SLOTS):
            offset_code = neighbours[block_row, :, slot_index]
            shift_z = offset_code // 3 - 1
            shift_y = offset_code % 3 - 1
            source_z = (block_row + shift_z) % blocks_z
            source_y = (column_ids + shift_y) % blocks_y
            other_pos = positions[source_z, source_y]
            other_rows = masked[source_z, source_y]
            weights = kernel_tile(own_pos, other_pos, shift_z.astype(jnp.float32), shift_y.astype(jnp.float32)).astype(jnp.bfloat16)
            total = total + jnp.einsum('bij,bjr->bir', weights.astype(jnp.float32), other_rows.astype(jnp.float32))
        return jnp.where(live_mask[block_row][..., None], total, jnp.zeros_like(total))
    image = lax.map(one_row, jnp.arange(blocks_z, dtype=jnp.int32))
    flat_rows = image.reshape(-1, SKETCH)
    gram = jnp.dot(flat_rows.T.astype(jnp.float32), flat_rows.astype(jnp.float32), preferred_element_type=jnp.float32, precision=lax.Precision.HIGHEST)
    lower_factor = jnp.linalg.cholesky(gram)
    solved = lax.linalg.triangular_solve(lower_factor, flat_rows.T, left_side=True, lower=True)
    scale_rows = math.sqrt(blocks_z * blocks_y * BLOCK_PTS)
    basis = (solved.T * scale_rows).reshape(blocks_z, blocks_y, BLOCK_PTS, SKETCH).astype(jnp.bfloat16)
    factor = lower_factor.T / scale_rows
    return (basis, factor)
```

```python
import functools
import math

import jax
import jax.numpy as jnp
from jax import lax
from jax.experimental import pallas as pl
from jax.experimental.pallas import tpu as pltpu
from jax.sharding import PartitionSpec as P

MESH = pl.DeviceIdType.MESH
HIGHEST = lax.Precision.HIGHEST
FAR = 100.0
SIDES = [(dz, dy) for dz in (-1, 0, 1) for dy in (-1, 0, 1) if (dz, dy) != (0, 0)]
VMEM = pl.BlockSpec(memory_space=pltpu.VMEM)
SMEM = pl.BlockSpec(memory_space=pltpu.SMEM)


def halo_kernel(slabs, grps, counts, pos, rows, wide_pos, wide_rows, send_p, recv_p, send_r, recv_r, own_sem):
    bz, by, dims, points = pos.shape
    slab, grp = lax.axis_index("slab"), lax.axis_index("grp")
    peers = [
        (lax.rem(slab + dz + slabs, slabs), lax.rem(grp + dy + grps, grps)) for dz, dy in SIDES
    ]
    barrier = pltpu.get_barrier_semaphore()
    for peer in peers:
        pl.semaphore_signal(barrier, inc=1, device_id=peer, device_id_type=MESH)
    own = pltpu.make_async_copy(rows, wide_rows.at[pl.ds(1, bz), pl.ds(1, by)], own_sem)
    own.start()
    ids = lax.broadcasted_iota(jnp.int32, (1, points), 1)
    for a in range(bz):
        for b in range(by):
            here = pos[a, b]
            far = jnp.where(ids < counts[a, b], here[0:1], FAR)
            wide_pos[a + 1, b + 1, 0:1, :] = far
            wide_pos[a + 1, b + 1, 1:3, :] = here[1:3]
            wide_pos[a + 1, b + 1, 3:8, :] = jnp.zeros((5, points), jnp.float32)
    pl.semaphore_wait(barrier, len(SIDES))

    def part(step, length):
        return {-1: (0, 1, length + 1), 0: (0, length, 1), 1: (length - 1, 1, 0)}[step]

    copies = []
    for k, (dz, dy) in enumerate(SIDES):
        z0, zn, zt = part(dz, bz)
        y0, yn, yt = part(dy, by)
        target = (pl.ds(zt, zn), pl.ds(yt, yn))
        copies.append(
            pltpu.make_async_remote_copy(
                src_ref=rows.at[pl.ds(z0, zn), pl.ds(y0, yn)],
                dst_ref=wide_rows.at[target],
                send_sem=send_r.at[k],
                recv_sem=recv_r.at[k],
                device_id=peers[k],
                device_id_type=MESH,
            )
        )
        copies.append(
            pltpu.make_async_remote_copy(
                src_ref=wide_pos.at[pl.ds(z0 + 1, zn), pl.ds(y0 + 1, yn)],
                dst_ref=wide_pos.at[target],
                send_sem=send_p.at[k],
                recv_sem=recv_p.at[k],
                device_id=peers[k],
                device_id_type=MESH,
            )
        )
    for copy in copies:
        copy.start()
    own.wait()
    for copy in copies:
        copy.wait()


def halo(positions, sketch, counts):
    bz, by, _, points = positions.shape
    columns = sketch.shape[3]
    kernel = functools.partial(halo_kernel, lax.axis_size("slab"), lax.axis_size("grp"))
    sides = len(SIDES)
    return pl.pallas_call(
        kernel,
        out_shape=(
            jax.ShapeDtypeStruct((bz + 2, by + 2, 8, points), jnp.float32),
            jax.ShapeDtypeStruct((bz + 2, by + 2, points, columns), sketch.dtype),
        ),
        in_specs=[SMEM, VMEM, VMEM],
        out_specs=(VMEM, VMEM),
        scratch_shapes=[pltpu.SemaphoreType.DMA((sides,))] * 4 + [pltpu.SemaphoreType.DMA],
        compiler_params=pltpu.CompilerParams(
            collective_id=0, has_side_effects=True, vmem_limit_bytes=32 << 20
        ),
        name="halo",
    )(counts, positions, sketch)


def image_kernel(neighbours, wide_pos, wide_rows, image, gram):
    bz, by = wide_pos.shape[0] - 2, wide_pos.shape[1] - 2
    points, columns = wide_rows.shape[2:]
    gram[...] = jnp.zeros_like(gram)

    def block_row(a, carry):
        def block(b, carry):
            own = wide_pos[a + 1, b + 1]
            turned = own.T
            own_z = jnp.where(turned[:, 0:1] > 0.5 * FAR, -FAR, turned[:, 0:1])
            own_y, own_x = turned[:, 1:2], turned[:, 2:3]
            total = jnp.zeros((points, columns), jnp.float32)
            for slot in range(neighbours.shape[2]):
                code = neighbours[a, b, slot]
                step_z = code // 3
                step_y = code - 3 * step_z
                other = wide_pos[a + step_z, b + step_y]
                diff_z = (other[0:1] + (step_z - 1).astype(jnp.float32)) - own_z
                diff_y = (other[1:2] + (step_y - 1).astype(jnp.float32)) - own_y
                diff_x = other[2:3] - own_x
                square = diff_z * diff_z + diff_y * diff_y + diff_x * diff_x
                radius = square * lax.rsqrt(jnp.maximum(square, 1e-30))
                taper = jnp.maximum(1.0 - radius, 0.0)
                taper = taper * taper
                tile = (taper * taper * (4.0 * radius + 1.0)).astype(jnp.bfloat16)
                total = total + jnp.dot(
                    tile, wide_rows[a + step_z, b + step_y], preferred_element_type=jnp.float32
                )
            image[pl.ds((a * by + b) * points, points), :] = total
            return carry

        lax.fori_loop(0, by, block, 0)
        part = image[pl.ds(a * by * points, by * points), :]
        gram[...] += lax.dot_general(
            part, part, (((0,), (0,)), ((), ())), precision=HIGHEST,
            preferred_element_type=jnp.float32,
        )
        return carry

    lax.fori_loop(0, bz, block_row, 0)


def make_image(neighbours, wide_pos, wide_rows):
    bz, by = neighbours.shape[:2]
    points, columns = wide_rows.shape[2:]
    return pl.pallas_call(
        image_kernel,
        out_shape=(
            jax.ShapeDtypeStruct((bz * by * points, columns), jnp.float32),
            jax.ShapeDtypeStruct((columns, columns), jnp.float32),
        ),
        in_specs=[SMEM, VMEM, VMEM],
        out_specs=(VMEM, VMEM),
        compiler_params=pltpu.CompilerParams(vmem_limit_bytes=32 << 20),
        name="image",
    )(neighbours, wide_pos, wide_rows)


def sum_kernel(slabs, grps, gram, out, held_g, part, held_s, *sems):
    n = gram.shape[0]
    wide = n // grps
    owners = min(slabs, wide // 8)
    narrow = wide // owners
    slab, grp = lax.axis_index("slab"), lax.axis_index("grp")
    send_1, recv_1, send_2, recv_2, send_3, recv_3, send_4, recv_4 = sems

    def grp_peer(off):
        return (slab, lax.rem(grp + off, grps))

    def slab_peer(off):
        return (lax.rem(slab + off, slabs), grp)

    barrier = pltpu.get_barrier_semaphore()
    for off in range(1, grps):
        pl.semaphore_signal(barrier, inc=1, device_id=grp_peer(off), device_id_type=MESH)
    for off in range(1, slabs):
        pl.semaphore_signal(barrier, inc=1, device_id=slab_peer(off), device_id_type=MESH)
    pl.semaphore_wait(barrier, grps + slabs - 2)

    def remote(src, dst, send, recv, off, peer):
        return pltpu.make_async_remote_copy(
            src_ref=src, dst_ref=dst, send_sem=send.at[off], recv_sem=recv.at[off],
            device_id=peer, device_id_type=MESH,
        )

    def rows_of(index, size):
        return pl.ds(pl.multiple_of(index * size, size), size)

    first = []
    for off in range(1, grps):
        peer = grp_peer(off)
        first.append(
            remote(gram.at[rows_of(peer[1], wide)], held_g.at[off], send_1, recv_1, off, peer)
        )
    for copy in first:
        copy.start()
    total = gram[rows_of(grp, wide), :]
    for off, copy in enumerate(first, 1):
        copy.wait_recv()
        total = total + held_g[off]
    part[...] = total

    mine = pl.ds(pl.multiple_of(grp * wide, wide), wide)

    def only(condition, body):
        if owners == slabs:
            body()
        else:
            pl.when(condition)(body)

    is_owner = slab < owners
    second = []
    for off in range(1, slabs):
        peer = slab_peer(off)
        place = lax.rem(peer[0], owners)
        second.append(
            remote(part.at[rows_of(place, narrow)], held_s.at[off], send_2, recv_2, off, peer)
        )
        only(peer[0] < owners, second[-1].start)

    place = lax.rem(slab, owners)
    strip = pl.ds(pl.multiple_of(grp * wide + place * narrow, narrow), narrow)
    third = [
        remote(out.at[strip], out.at[strip], send_3, recv_3, off, slab_peer(off))
        for off in range(1, slabs)
    ]

    def add_up():
        total = part[rows_of(place, narrow), :]
        for off, copy in enumerate(second, 1):
            copy.wait_recv()
            total = total + held_s[off]
        out[strip, :] = total
        for copy in third:
            copy.start()

    only(is_owner, add_up)
    for off, copy in enumerate(third, 1):
        only(lax.rem(slab - off + slabs, slabs) < owners, copy.wait_recv)

    fourth = [
        remote(out.at[mine], out.at[mine], send_4, recv_4, off, grp_peer(off))
        for off in range(1, grps)
    ]
    for copy in fourth:
        copy.start()
    for copy in first:
        copy.wait_send()
    for off, copy in enumerate(second, 1):
        only(slab_peer(off)[0] < owners, copy.wait_send)
    for copy in third:
        only(is_owner, copy.wait_send)
    for copy in fourth:
        copy.wait()


def sum_over_devices(gram):
    slabs, grps = lax.axis_size("slab"), lax.axis_size("grp")
    n = gram.shape[0]
    wide = n // grps
    narrow = wide // min(slabs, wide // 8)
    dma = pltpu.SemaphoreType.DMA
    return pl.pallas_call(
        functools.partial(sum_kernel, slabs, grps),
        out_shape=jax.ShapeDtypeStruct((n, n), jnp.float32),
        in_specs=[VMEM],
        out_specs=VMEM,
        scratch_shapes=[
            pltpu.VMEM((grps, wide, n), jnp.float32),
            pltpu.VMEM((wide, n), jnp.float32),
            pltpu.VMEM((slabs, narrow, n), jnp.float32),
        ]
        + [dma((grps,)), dma((grps,))]
        + [dma((slabs,))] * 4
        + [dma((grps,)), dma((grps,))],
        compiler_params=pltpu.CompilerParams(
            collective_id=1, has_side_effects=True, vmem_limit_bytes=32 << 20
        ),
        name="gram_sum",
    )(gram)


HEIGHT = 32
GROUP = 8


def factor_kernel(scale, gram, image, basis, factor, work):
    n = gram.shape[0]
    half = n // 2
    row_ids = lax.broadcasted_iota(jnp.int32, (n, n), 0)
    col_ids = lax.broadcasted_iota(jnp.int32, (n, n), 1)
    work[:, 0:n] = gram[...]
    work[:, n : 2 * n] = jnp.where(row_ids == col_ids, 1.0, 0.0)
    for base in range(0, n, HEIGHT):
        lane0 = 0 if base < half else half
        tiles = [
            work[base : base + HEIGHT, lane0 + half * t : lane0 + half * (t + 1)] for t in range(3)
        ]
        ids = lax.broadcasted_iota(jnp.int32, (HEIGHT, half), 0)
        scales = jnp.zeros((HEIGHT, half), jnp.float32)
        for start in range(0, HEIGHT, GROUP):
            col0 = base - lane0 + start
            spread = [
                jnp.broadcast_to(tiles[0][start:, col0 + j : col0 + j + 1], (HEIGHT - start, half))
                for j in range(GROUP)
            ]
            done = [t[:start] for t in tiles]
            live = [t[start:] for t in tiles]
            live_ids = ids[start:]
            for p in range(GROUP):
                pivot = spread[p][p : p + 1]
                scales = jnp.where(ids == start + p, lax.rsqrt(pivot), scales)
                ratio = jnp.where(live_ids > start + p, spread[p] * (1.0 / pivot), 0.0)
                for j in range(p + 1, GROUP):
                    spread[j] = spread[j] - ratio * spread[j][p : p + 1]
                live = [t - ratio * t[p : p + 1] for t in live]
            tiles = [
                jnp.concatenate([d, t], axis=0) if start else t for d, t in zip(done, live)
            ]
        tiles = [t * scales for t in tiles]
        for t in range(3):
            work[base : base + HEIGHT, lane0 + half * t : lane0 + half * (t + 1)] = tiles[t]
        after = base + HEIGHT
        if after < n:
            right = jnp.concatenate(tiles, axis=1)
            left = jnp.concatenate(tiles[:2], axis=1) if base < half else tiles[0]
            change = lax.dot_general(
                left, right, (((0,), (0,)), ((), ())), precision=HIGHEST,
                preferred_element_type=jnp.float32,
            )
            work[after:n, lane0 : lane0 + 3 * half] -= change[after - lane0 :]
    factor[...] = jnp.where(col_ids >= row_ids, work[:, 0:n], 0.0) * (1.0 / scale)
    inverse = work[:, n : 2 * n] * scale
    rows = image.shape[0]
    chunk = min(rows, 512)

    def solve(i, carry):
        here = pl.ds(pl.multiple_of(i * chunk, chunk), chunk)
        basis[here, :] = lax.dot_general(
            image[here, :], inverse, (((1,), (1,)), ((), ())), precision=HIGHEST,
            preferred_element_type=jnp.float32,
        ).astype(basis.dtype)
        return carry

    lax.fori_loop(0, rows // chunk, solve, 0)


def factor_and_basis(gram, image, scale):
    rows, n = image.shape
    return pl.pallas_call(
        functools.partial(factor_kernel, scale),
        out_shape=(
            jax.ShapeDtypeStruct((rows, n), jnp.bfloat16),
            jax.ShapeDtypeStruct((n, n), jnp.float32),
        ),
        in_specs=[VMEM, VMEM],
        out_specs=(VMEM, VMEM),
        scratch_shapes=[pltpu.VMEM((n, 2 * n), jnp.float32)],
        compiler_params=pltpu.CompilerParams(vmem_limit_bytes=32 << 20),
        name="factor",
    )(gram, image)


def on_device(positions, sketch, counts, neighbours):
    blocks_z, blocks_y, _, points = positions.shape
    columns = sketch.shape[3]
    wide_pos, wide_rows = halo(positions, sketch, counts)
    image, gram = make_image(neighbours, wide_pos, wide_rows)
    gram = sum_over_devices(gram)
    total_rows = lax.axis_size("slab") * blocks_z * lax.axis_size("grp") * blocks_y * points
    basis, factor = factor_and_basis(gram, image, math.sqrt(total_rows))
    return basis.reshape(blocks_z, blocks_y, points, columns), factor


def solution(mesh):
    placed = (
        P("slab", "grp", None, None),
        P("slab", "grp", None, None),
        P("slab", "grp"),
        P("slab", "grp", None),
    )
    return jax.shard_map(
        on_device,
        mesh=mesh,
        in_specs=placed,
        out_specs=(P("slab", "grp", None, None), P()),
        check_vma=False,
    )
```

```python
import functools
import math

import jax
import jax.numpy as jnp
from jax import lax
from jax.experimental import pallas as pl
from jax.experimental.pallas import tpu as pltpu
from jax.sharding import PartitionSpec as P

MESH = pl.DeviceIdType.MESH
HIGHEST = lax.Precision.HIGHEST
FAR = 100.0
VMEM = pl.BlockSpec(memory_space=pltpu.VMEM)
SMEM = pl.BlockSpec(memory_space=pltpu.SMEM)


def main_kernel(slabs, grps, counts, neighbours, pos, rows, image, out, wide_pos, wide_rows, cols, gram,
                held_g, part, held_s, own_sem, *sems):
    bz, by, dims, points = pos.shape
    columns = rows.shape[3]
    halo_sems, sems = sems[:8], sems[8:]
    slab, grp = lax.axis_index("slab"), lax.axis_index("grp")

    def grp_peer(off):
        return (slab, lax.rem(grp + off, grps))

    def slab_peer(off):
        return (lax.rem(slab + off, slabs), grp)

    barrier = pltpu.get_barrier_semaphore()
    for off in range(1, grps):
        pl.semaphore_signal(barrier, inc=1, device_id=grp_peer(off), device_id_type=MESH)
    for off in range(1, slabs):
        pl.semaphore_signal(barrier, inc=1, device_id=slab_peer(off), device_id_type=MESH)
    own_rows = pltpu.make_async_copy(rows, wide_rows.at[pl.ds(1, bz), pl.ds(1, by)], own_sem)
    own_rows.start()
    ids = lax.broadcasted_iota(jnp.int32, (1, points), 1)
    for a in range(bz):
        for b in range(by):
            far = jnp.where(ids < counts[a, b], pos[a, b, 0:1], FAR)
            wide_pos[a + 1, b + 1, 0:1, :] = far
            wide_pos[a + 1, b + 1, 1:3, :] = pos[a, b, 1:3]
            wide_pos[a + 1, b + 1, 3:8, :] = jnp.zeros((5, points), jnp.float32)
    own_rows.wait()
    pl.semaphore_wait(barrier, grps + slabs - 2)

    def remote(src, dst, send, recv, peer):
        return pltpu.make_async_remote_copy(
            src_ref=src, dst_ref=dst, send_sem=send, recv_sem=recv,
            device_id=peer, device_id_type=MESH,
        )

    def both(kind, k, src, dst, peer):
        send_r, recv_r, send_p, recv_p = halo_sems[4 * kind : 4 * kind + 4]
        return [
            remote(wide_pos.at[src], wide_pos.at[dst], send_p.at[k], recv_p.at[k], peer),
            remote(wide_rows.at[src], wide_rows.at[dst], send_r.at[k], recv_r.at[k], peer),
        ]

    inner_z, inner_y = pl.ds(1, bz), pl.ds(1, by)
    up, down = slab_peer(1), slab_peer(slabs - 1)
    right, left = grp_peer(1), grp_peer(grps - 1)
    slab_copies = both(0, 0, (pl.ds(bz, 1), inner_y), (pl.ds(0, 1), inner_y), up)
    slab_copies += both(0, 1, (pl.ds(1, 1), inner_y), (pl.ds(bz + 1, 1), inner_y), down)
    grp_copies = both(0, 2, (inner_z, pl.ds(by, 1)), (inner_z, pl.ds(0, 1)), right)
    grp_copies += both(0, 3, (inner_z, pl.ds(1, 1)), (inner_z, pl.ds(by + 1, 1)), left)
    for copy in slab_copies + grp_copies:
        copy.start()

    def turn(i, carry):
        turned = wide_pos[i // by + 1, i % by + 1].T
        own_z = turned[:, 0:1]
        cols[i, 0] = jnp.broadcast_to(jnp.where(own_z > 0.5 * FAR, -FAR, own_z), (points, points))
        cols[i, 1] = jnp.broadcast_to(turned[:, 1:2], (points, points))
        cols[i, 2] = jnp.broadcast_to(turned[:, 2:3], (points, points))
        image[pl.ds(i * points, points), :] = jnp.zeros((points, columns), jnp.float32)
        return carry

    lax.fori_loop(0, bz * by, turn, 0)
    gram[...] = jnp.zeros_like(gram)

    def dropped(a, b):
        total = neighbours[a, b, 0]
        for slot in range(1, neighbours.shape[2]):
            total = total + neighbours[a, b, slot]
        return 36 - total

    def tile(a, b, dz, dy, skip):
        code = 3 * (dz + 1) + dy + 1
        shift_z = jnp.where(skip == code, 10.0 * FAR, jnp.asarray(dz).astype(jnp.float32))
        other = wide_pos[a + dz + 1, b + dy + 1]
        own = a * by + b
        diff_z = (other[0:1] + shift_z) - cols[own, 0]
        diff_y = (other[1:2] + float(dy)) - cols[own, 1]
        diff_x = other[2:3] - cols[own, 2]
        square = diff_z * diff_z + diff_y * diff_y + diff_x * diff_x
        radius = square * lax.rsqrt(jnp.maximum(square, 1e-30))
        taper = jnp.maximum(1.0 - radius, 0.0)
        taper = taper * taper
        return (taper * taper * (4.0 * radius + 1.0)).astype(jnp.bfloat16)

    def add_to(a, b, tiles, sources):
        here = pl.ds((a * by + b) * points, points)
        image[here, :] += jnp.dot(
            jnp.concatenate(tiles, axis=1),
            sources.reshape(len(tiles) * points, columns),
            preferred_element_type=jnp.float32,
        )

    def one_row(t, carry):
        dz, a = t // bz - 1, t % bz
        for b in range(by):
            skip = dropped(a, b)
            steps = [dy for dy in (-1, 0, 1) if 0 <= b + dy < by]
            tiles = [tile(a, b, dz, dy, skip) for dy in steps]
            first = b + steps[0] + 1
            add_to(a, b, tiles, wide_rows[a + dz + 1, first : first + len(steps)])
        return carry

    lax.fori_loop(1, 3 * bz - 1, one_row, 0)

    for copy in slab_copies:
        copy.wait_recv()
    corners = []
    for k, z in enumerate((0, bz + 1)):
        row = pl.ds(z, 1)
        corners += both(1, 2 * k, (row, pl.ds(by, 1)), (row, pl.ds(0, 1)), right)
        corners += both(1, 2 * k + 1, (row, pl.ds(1, 1)), (row, pl.ds(by + 1, 1)), left)
    for copy in corners:
        copy.start()

    lax.fori_loop(0, 2, lambda i, carry: one_row(i * (3 * bz - 1), carry), 0)

    for copy in grp_copies + corners:
        copy.wait_recv()

    def outer(a, carry):
        for b, dy in ((0, -1), (by - 1, 1)):
            skip = dropped(a, b)
            tiles = [tile(a, b, dz, dy, skip) for dz in (-1, 0, 1)]
            add_to(a, b, tiles, wide_rows[pl.ds(a, 3), b + dy + 1])
        band = image[pl.ds(a * by * points, by * points), :]
        gram[...] += lax.dot_general(
            band, band, (((0,), (0,)), ((), ())), precision=HIGHEST,
            preferred_element_type=jnp.float32,
        )
        return carry

    lax.fori_loop(0, bz, outer, 0)
    sum_gram(slabs, grps, slab, grp, grp_peer, slab_peer, gram, out, held_g, part, held_s, sems)
    for copy in slab_copies + grp_copies + corners:
        copy.wait_send()


def sum_gram(slabs, grps, slab, grp, grp_peer, slab_peer, gram, out, held_g, part, held_s, sems):
    n = gram.shape[0]
    wide = n // grps
    owners = min(slabs, wide // 8)
    narrow = wide // owners
    send_1, recv_1, send_2, recv_2, send_3, recv_3, send_4, recv_4 = sems

    def remote(src, dst, send, recv, off, peer):
        return pltpu.make_async_remote_copy(
            src_ref=src, dst_ref=dst, send_sem=send.at[off], recv_sem=recv.at[off],
            device_id=peer, device_id_type=MESH,
        )

    def rows_of(index, size):
        return pl.ds(pl.multiple_of(index * size, size), size)

    first = []
    for off in range(1, grps):
        peer = grp_peer(off)
        first.append(
            remote(gram.at[rows_of(peer[1], wide)], held_g.at[off], send_1, recv_1, off, peer)
        )
    for copy in first:
        copy.start()
    total = gram[rows_of(grp, wide), :]
    for off, copy in enumerate(first, 1):
        copy.wait_recv()
        total = total + held_g[off]
    part[...] = total

    mine = pl.ds(pl.multiple_of(grp * wide, wide), wide)

    def only(condition, body):
        if owners == slabs:
            body()
        else:
            pl.when(condition)(body)

    is_owner = slab < owners
    second = []
    for off in range(1, slabs):
        peer = slab_peer(off)
        place = lax.rem(peer[0], owners)
        second.append(
            remote(part.at[rows_of(place, narrow)], held_s.at[off], send_2, recv_2, off, peer)
        )
        only(peer[0] < owners, second[-1].start)

    place = lax.rem(slab, owners)
    strip = pl.ds(pl.multiple_of(grp * wide + place * narrow, narrow), narrow)
    third = [
        remote(out.at[strip], out.at[strip], send_3, recv_3, off, slab_peer(off))
        for off in range(1, slabs)
    ]

    def add_up():
        total = part[rows_of(place, narrow), :]
        for off, copy in enumerate(second, 1):
            copy.wait_recv()
            total = total + held_s[off]
        out[strip, :] = total
        for copy in third:
            copy.start()

    only(is_owner, add_up)
    for off, copy in enumerate(third, 1):
        only(lax.rem(slab - off + slabs, slabs) < owners, copy.wait_recv)

    fourth = [
        remote(out.at[mine], out.at[mine], send_4, recv_4, off, grp_peer(off))
        for off in range(1, grps)
    ]
    for copy in fourth:
        copy.start()
    for copy in first:
        copy.wait_send()
    for off, copy in enumerate(second, 1):
        only(slab_peer(off)[0] < owners, copy.wait_send)
    for copy in third:
        only(is_owner, copy.wait_send)
    for copy in fourth:
        copy.wait()


def image_and_gram(positions, sketch, counts, neighbours):
    slabs, grps = lax.axis_size("slab"), lax.axis_size("grp")
    bz, by, _, points = positions.shape
    n = sketch.shape[3]
    wide = n // grps
    narrow = wide // min(slabs, wide // 8)
    dma = pltpu.SemaphoreType.DMA
    vmem = pltpu.VMEM
    return pl.pallas_call(
        functools.partial(main_kernel, slabs, grps),
        out_shape=(
            jax.ShapeDtypeStruct((bz * by * points, n), jnp.float32),
            jax.ShapeDtypeStruct((n, n), jnp.float32),
        ),
        in_specs=[SMEM, SMEM, VMEM, pl.BlockSpec(memory_space=pl.ANY)],
        out_specs=(VMEM, VMEM),
        scratch_shapes=[
            vmem((bz + 2, by + 2, 8, points), jnp.float32),
            vmem((bz + 2, by + 2, points, n), sketch.dtype),
            vmem((bz * by, 3, points, points), jnp.float32),
            vmem((n, n), jnp.float32),
            vmem((grps, wide, n), jnp.float32),
            vmem((wide, n), jnp.float32),
            vmem((slabs, narrow, n), jnp.float32),
            dma,
        ]
        + [dma((4,))] * 8
        + [dma((grps,)), dma((grps,))]
        + [dma((slabs,))] * 4
        + [dma((grps,)), dma((grps,))],
        compiler_params=pltpu.CompilerParams(
            collective_id=0, has_side_effects=True, vmem_limit_bytes=40 << 20
        ),
        name="image_gram",
    )(counts, neighbours, positions, sketch)


HEIGHT = 32
GROUP = 8


def factor_kernel(scale, gram, image, basis, factor, work):
    n = gram.shape[0]
    half = n // 2
    row_ids = lax.broadcasted_iota(jnp.int32, (n, n), 0)
    col_ids = lax.broadcasted_iota(jnp.int32, (n, n), 1)
    work[:, 0:n] = gram[...]
    work[:, n : 2 * n] = jnp.where(row_ids == col_ids, 1.0, 0.0)
    for base in range(0, n, HEIGHT):
        lane0 = 0 if base < half else half
        tiles = [
            work[base : base + HEIGHT, lane0 + half * t : lane0 + half * (t + 1)] for t in range(3)
        ]
        ids = lax.broadcasted_iota(jnp.int32, (HEIGHT, half), 0)
        scales = jnp.zeros((HEIGHT, half), jnp.float32)
        for start in range(0, HEIGHT, GROUP):
            col0 = base - lane0 + start
            spread = [
                jnp.broadcast_to(tiles[0][start:, col0 + j : col0 + j + 1], (HEIGHT - start, half))
                for j in range(GROUP)
            ]
            done = [t[:start] for t in tiles]
            live = [t[start:] for t in tiles]
            live_ids = ids[start:]
            for p in range(GROUP):
                pivot = spread[p][p : p + 1]
                scales = jnp.where(ids == start + p, lax.rsqrt(pivot), scales)
                ratio = jnp.where(live_ids > start + p, spread[p] * (1.0 / pivot), 0.0)
                for j in range(p + 1, GROUP):
                    spread[j] = spread[j] - ratio * spread[j][p : p + 1]
                live = [t - ratio * t[p : p + 1] for t in live]
            tiles = [
                jnp.concatenate([d, t], axis=0) if start else t for d, t in zip(done, live)
            ]
        tiles = [t * scales for t in tiles]
        for t in range(3):
            work[base : base + HEIGHT, lane0 + half * t : lane0 + half * (t + 1)] = tiles[t]
        after = base + HEIGHT
        if after < n:
            right = jnp.concatenate(tiles, axis=1)
            left = jnp.concatenate(tiles[:2], axis=1) if base < half else tiles[0]
            change = lax.dot_general(
                left, right, (((0,), (0,)), ((), ())), precision=HIGHEST,
                preferred_element_type=jnp.float32,
            )
            work[after:n, lane0 : lane0 + 3 * half] -= change[after - lane0 :]
    factor[...] = jnp.where(col_ids >= row_ids, work[:, 0:n], 0.0) * (1.0 / scale)
    inverse = work[:, n : 2 * n] * scale
    rows = image.shape[0]
    chunk = min(rows, 512)

    def solve(i, carry):
        here = pl.ds(pl.multiple_of(i * chunk, chunk), chunk)
        basis[here, :] = lax.dot_general(
            image[here, :], inverse, (((1,), (1,)), ((), ())), precision=HIGHEST,
            preferred_element_type=jnp.float32,
        ).astype(basis.dtype)
        return carry

    lax.fori_loop(0, rows // chunk, solve, 0)


def factor_and_basis(gram, image, scale):
    rows, n = image.shape
    return pl.pallas_call(
        functools.partial(factor_kernel, scale),
        out_shape=(
            jax.ShapeDtypeStruct((rows, n), jnp.bfloat16),
            jax.ShapeDtypeStruct((n, n), jnp.float32),
        ),
        in_specs=[VMEM, VMEM],
        out_specs=(VMEM, VMEM),
        scratch_shapes=[pltpu.VMEM((n, 2 * n), jnp.float32)],
        compiler_params=pltpu.CompilerParams(vmem_limit_bytes=32 << 20),
        name="factor",
    )(gram, image)


def on_device(positions, sketch, counts, neighbours):
    blocks_z, blocks_y, _, points = positions.shape
    columns = sketch.shape[3]
    image, gram = image_and_gram(positions, sketch, counts, neighbours)
    total_rows = lax.axis_size("slab") * blocks_z * lax.axis_size("grp") * blocks_y * points
    basis, factor = factor_and_basis(gram, image, math.sqrt(total_rows))
    return basis.reshape(blocks_z, blocks_y, points, columns), factor


def solution(mesh):
    placed = (
        P("slab", "grp", None, None),
        P("slab", "grp", None, None),
        P("slab", "grp"),
        P("slab", "grp", None),
    )
    return jax.shard_map(
        on_device,
        mesh=mesh,
        in_specs=placed,
        out_specs=(P("slab", "grp", None, None), P()),
        check_vma=False,
    )
```

```python
import functools
import math

import jax
import jax.numpy as jnp
from jax import lax
from jax.experimental import pallas as pl
from jax.experimental.pallas import tpu as pltpu
from jax.sharding import PartitionSpec as P

MESH = pl.DeviceIdType.MESH
HIGHEST = lax.Precision.HIGHEST
FAR = 100.0
VMEM = pl.BlockSpec(memory_space=pltpu.VMEM)
SMEM = pl.BlockSpec(memory_space=pltpu.SMEM)


def two_parts(x):
    high = x.astype(jnp.bfloat16)
    return high, (x - high.astype(jnp.float32)).astype(jnp.bfloat16)


def turned_dot(x, y):
    return lax.dot_general(x, y, (((0,), (0,)), ((), ())), preferred_element_type=jnp.float32)


def dot_turned(x, y):
    return lax.dot_general(x, y, (((1,), (1,)), ((), ())), preferred_element_type=jnp.float32)


def main_kernel(slabs, grps, counts, neighbours, pos, rows, image, out, wide_pos, wide_rows, own_parts, other_parts, gram, cross,
                held_g, part, held_s, own_sem, *sems):
    bz, by, dims, points = pos.shape
    columns = rows.shape[3]
    halo_sems, sems = sems[:8], sems[8:]
    slab, grp = lax.axis_index("slab"), lax.axis_index("grp")

    def grp_peer(off):
        return (slab, lax.rem(grp + off, grps))

    def slab_peer(off):
        return (lax.rem(slab + off, slabs), grp)

    barrier = pltpu.get_barrier_semaphore()
    for off in range(1, grps):
        pl.semaphore_signal(barrier, inc=1, device_id=grp_peer(off), device_id_type=MESH)
    for off in range(1, slabs):
        pl.semaphore_signal(barrier, inc=1, device_id=slab_peer(off), device_id_type=MESH)
    own_rows = pltpu.make_async_copy(rows, wide_rows.at[pl.ds(1, bz), pl.ds(1, by)], own_sem)
    own_rows.start()
    ids = lax.broadcasted_iota(jnp.int32, (1, points), 1)
    for a in range(bz):
        for b in range(by):
            far = jnp.where(ids < counts[a, b], pos[a, b, 0:1], FAR)
            wide_pos[a + 1, b + 1, 0:1, :] = far
            wide_pos[a + 1, b + 1, 1:3, :] = pos[a, b, 1:3]
            wide_pos[a + 1, b + 1, 3:8, :] = jnp.zeros((5, points), jnp.float32)
    own_rows.wait()
    pl.semaphore_wait(barrier, grps + slabs - 2)

    def remote(src, dst, send, recv, peer):
        return pltpu.make_async_remote_copy(
            src_ref=src, dst_ref=dst, send_sem=send, recv_sem=recv,
            device_id=peer, device_id_type=MESH,
        )

    def both(kind, k, src, dst, peer):
        send_r, recv_r, send_p, recv_p = halo_sems[4 * kind : 4 * kind + 4]
        return [
            remote(wide_pos.at[src], wide_pos.at[dst], send_p.at[k], recv_p.at[k], peer),
            remote(wide_rows.at[src], wide_rows.at[dst], send_r.at[k], recv_r.at[k], peer),
        ]

    inner_z, inner_y = pl.ds(1, bz), pl.ds(1, by)
    up, down = slab_peer(1), slab_peer(slabs - 1)
    right, left = grp_peer(1), grp_peer(grps - 1)
    ends, middles = [], []
    for k, source, target, peer in ((0, bz, 0, up), (3, 1, bz + 1, down)):
        for at, copies, y in (
            (0, ends, pl.ds(1, 1)), (1, ends, pl.ds(by, 1)), (2, middles, pl.ds(2, by - 2))
        ):
            copies += both(0, k + at, (pl.ds(source, 1), y), (pl.ds(target, 1), y), peer)
    grp_copies = both(0, 6, (inner_z, pl.ds(by, 1)), (inner_z, pl.ds(0, 1)), right)
    grp_copies += both(0, 7, (inner_z, pl.ds(1, 1)), (inner_z, pl.ds(by + 1, 1)), left)
    for copy in ends + middles + grp_copies:
        copy.start()

    part_rows = lax.broadcasted_iota(jnp.int32, (8, points), 0)

    def split(z, y):
        here = wide_pos[z, y]
        mid_z = (jnp.asarray(z) - 1 - bz // 2).astype(jnp.float32)
        mid_y = (jnp.asarray(y) - 1 - by // 2).astype(jnp.float32)
        moved = here + jnp.where(part_rows == 0, mid_z, jnp.where(part_rows == 1, mid_y, -0.5))
        empty = here[0:1] > 0.5 * FAR
        moved = jnp.where((part_rows < 3) & jnp.logical_not(empty), moved, 0.0)
        norm = jnp.where(empty, 1000.0, jnp.sum(moved * moved, axis=0, keepdims=True))
        whole = jnp.where(part_rows == 3, norm, moved)
        high = whole.astype(jnp.bfloat16).astype(jnp.float32)
        rest = whole - high
        middle = rest.astype(jnp.bfloat16).astype(jnp.float32)
        return high, middle, rest - middle

    def stack(parts, norms):
        merged = [jnp.where(part_rows == 3, n, p) for p, n in zip(parts, norms)]
        return jnp.concatenate(merged, axis=0)

    def put_other(z, y):
        h, m, low = split(z, y)
        parts = [-2.0 * p for p in (h, m, h, m, low, h)]
        other_parts[z, y] = stack(parts, (1.0, 1.0, 1.0, h, m, low)).astype(jnp.bfloat16)
        return h, m, low

    def turn(a, carry):
        for b in range(by):
            h, m, low = put_other(a + 1, b + 1)
            mine = stack((h, h, m, m, h, low), (h, m, low, 1.0, 1.0, 1.0))
            own_parts[a * by + b] = mine.T.astype(jnp.bfloat16)
        band = pl.ds(a * by * points, by * points)
        image[band, :] = jnp.zeros((by * points, columns), jnp.float32)
        return carry

    lax.fori_loop(0, bz, turn, 0)
    gram[...] = jnp.zeros_like(gram)
    cross[...] = jnp.zeros_like(cross)

    def dropped(a, b):
        total = neighbours[a, b, 0]
        for slot in range(1, neighbours.shape[2]):
            total = total + neighbours[a, b, slot]
        return 36 - total

    def tile(a, b, dz, dy, skip):
        code = 3 * (dz + 1) + dy + 1
        least = jnp.where(skip == code, 4.0, 1e-30)
        square = jnp.dot(
            own_parts[a * by + b], other_parts[a + dz + 1, b + dy + 1],
            preferred_element_type=jnp.float32,
        )
        square = jnp.maximum(square, least)
        radius = square * lax.rsqrt(square)
        taper = jnp.maximum(1.0 - radius, 0.0)
        taper = taper * taper
        return (taper * taper * (4.0 * radius + 1.0)).astype(jnp.bfloat16)

    def add_to(a, b, tiles, sources):
        here = pl.ds((a * by + b) * points, points)
        image[here, :] += jnp.dot(
            jnp.concatenate(tiles, axis=1),
            sources.reshape(len(tiles) * points, columns),
            preferred_element_type=jnp.float32,
        )

    def one_row(t, carry):
        dz, a = t // bz - 1, t % bz
        for b in range(by):
            skip = dropped(a, b)
            steps = [dy for dy in (-1, 0, 1) if 0 <= b + dy < by]
            tiles = [tile(a, b, dz, dy, skip) for dy in steps]
            first = b + steps[0] + 1
            add_to(a, b, tiles, wide_rows[a + dz + 1, first : first + len(steps)])
        return carry

    lax.fori_loop(1, bz + 1, one_row, 0)

    for copy in ends:
        copy.wait_recv()
    corners = []
    for k, z in enumerate((0, bz + 1)):
        row = pl.ds(z, 1)
        corners += both(1, 2 * k, (row, pl.ds(by, 1)), (row, pl.ds(0, 1)), right)
        corners += both(1, 2 * k + 1, (row, pl.ds(1, 1)), (row, pl.ds(by + 1, 1)), left)
    for copy in corners:
        copy.start()
    lax.fori_loop(bz + 1, 3 * bz - 1, one_row, 0)

    for copy in middles:
        copy.wait_recv()
    for y in range(1, by + 1):
        put_other(0, y)
        put_other(bz + 1, y)

    lax.fori_loop(0, 2, lambda i, carry: one_row(i * (3 * bz - 1), carry), 0)

    for copy in grp_copies + corners:
        copy.wait_recv()
    for z in range(bz + 2):
        put_other(z, 0)
        put_other(z, by + 1)

    def outer(a, carry):
        for b, dy in ((0, -1), (by - 1, 1)):
            skip = dropped(a, b)
            tiles = [tile(a, b, dz, dy, skip) for dz in (-1, 0, 1)]
            add_to(a, b, tiles, wide_rows[pl.ds(a, 3), b + dy + 1])
        band = image[pl.ds(a * by * points, by * points), :]
        high, low = two_parts(band)
        gram[...] += turned_dot(high, high) + turned_dot(low, low)
        cross[...] += turned_dot(high, low)
        return carry

    lax.fori_loop(0, bz, outer, 0)
    gram[...] += cross[...] + cross[...].T
    sum_gram(slabs, grps, slab, grp, grp_peer, slab_peer, gram, out, held_g, part, held_s, sems)
    for copy in ends + middles + grp_copies + corners:
        copy.wait_send()


def sum_gram(slabs, grps, slab, grp, grp_peer, slab_peer, gram, out, held_g, part, held_s, sems):
    n = gram.shape[0]
    wide = n // grps
    owners = min(slabs, wide // 8)
    narrow = wide // owners
    send_1, recv_1, send_2, recv_2, send_3, recv_3, send_4, recv_4 = sems

    def remote(src, dst, send, recv, off, peer):
        return pltpu.make_async_remote_copy(
            src_ref=src, dst_ref=dst, send_sem=send.at[off], recv_sem=recv.at[off],
            device_id=peer, device_id_type=MESH,
        )

    def rows_of(index, size):
        return pl.ds(pl.multiple_of(index * size, size), size)

    first = []
    for off in range(1, grps):
        peer = grp_peer(off)
        first.append(
            remote(gram.at[rows_of(peer[1], wide)], held_g.at[off], send_1, recv_1, off, peer)
        )
    for copy in first:
        copy.start()
    total = gram[rows_of(grp, wide), :]
    for off, copy in enumerate(first, 1):
        copy.wait_recv()
        total = total + held_g[off]
    part[...] = total

    mine = pl.ds(pl.multiple_of(grp * wide, wide), wide)

    def only(condition, body):
        if owners == slabs:
            body()
        else:
            pl.when(condition)(body)

    is_owner = slab < owners
    second = []
    for off in range(1, slabs):
        peer = slab_peer(off)
        place = lax.rem(peer[0], owners)
        second.append(
            remote(part.at[rows_of(place, narrow)], held_s.at[off], send_2, recv_2, off, peer)
        )
        only(peer[0] < owners, second[-1].start)

    place = lax.rem(slab, owners)
    strip = pl.ds(pl.multiple_of(grp * wide + place * narrow, narrow), narrow)
    third = [
        remote(out.at[strip], out.at[strip], send_3, recv_3, off, slab_peer(off))
        for off in range(1, slabs)
    ]

    def add_up():
        total = part[rows_of(place, narrow), :]
        for off, copy in enumerate(second, 1):
            copy.wait_recv()
            total = total + held_s[off]
        out[strip, :] = total
        for copy in third:
            copy.start()

    only(is_owner, add_up)
    for off, copy in enumerate(third, 1):
        only(lax.rem(slab - off + slabs, slabs) < owners, copy.wait_recv)

    fourth = [
        remote(out.at[mine], out.at[mine], send_4, recv_4, off, grp_peer(off))
        for off in range(1, grps)
    ]
    for copy in fourth:
        copy.start()
    for copy in first:
        copy.wait_send()
    for off, copy in enumerate(second, 1):
        only(slab_peer(off)[0] < owners, copy.wait_send)
    for copy in third:
        only(is_owner, copy.wait_send)
    for copy in fourth:
        copy.wait()


def image_and_gram(positions, sketch, counts, neighbours):
    slabs, grps = lax.axis_size("slab"), lax.axis_size("grp")
    bz, by, _, points = positions.shape
    n = sketch.shape[3]
    wide = n // grps
    narrow = wide // min(slabs, wide // 8)
    dma = pltpu.SemaphoreType.DMA
    vmem = pltpu.VMEM
    return pl.pallas_call(
        functools.partial(main_kernel, slabs, grps),
        out_shape=(
            jax.ShapeDtypeStruct((bz * by * points, n), jnp.float32),
            jax.ShapeDtypeStruct((n, n), jnp.float32),
        ),
        in_specs=[SMEM, SMEM, VMEM, pl.BlockSpec(memory_space=pl.ANY)],
        out_specs=(VMEM, VMEM),
        scratch_shapes=[
            vmem((bz + 2, by + 2, 8, points), jnp.float32),
            vmem((bz + 2, by + 2, points, n), sketch.dtype),
            vmem((bz * by, points, 48), jnp.bfloat16),
            vmem((bz + 2, by + 2, 48, points), jnp.bfloat16),
            vmem((n, n), jnp.float32),
            vmem((n, n), jnp.float32),
            vmem((grps, wide, n), jnp.float32),
            vmem((wide, n), jnp.float32),
            vmem((slabs, narrow, n), jnp.float32),
            dma,
        ]
        + [dma((8,))] * 8
        + [dma((grps,)), dma((grps,))]
        + [dma((slabs,))] * 4
        + [dma((grps,)), dma((grps,))],
        compiler_params=pltpu.CompilerParams(
            collective_id=0, has_side_effects=True, vmem_limit_bytes=40 << 20
        ),
        name="image_gram",
    )(counts, neighbours, positions, sketch)


HEIGHT = 64
GROUP = 8


def factor_kernel(scale, gram, image, basis, factor, work):
    n = gram.shape[0]
    half = n // 2
    row_ids = lax.broadcasted_iota(jnp.int32, (n, n), 0)
    col_ids = lax.broadcasted_iota(jnp.int32, (n, n), 1)
    work[:, 0:n] = gram[...]
    work[:, n : 2 * n] = jnp.where(row_ids == col_ids, 1.0, 0.0)
    for base in range(0, n, HEIGHT):
        lane0 = 0 if base < half else half
        tiles = [
            work[base : base + HEIGHT, lane0 + half * t : lane0 + half * (t + 1)] for t in range(3)
        ]
        ids = lax.broadcasted_iota(jnp.int32, (HEIGHT, half), 0)
        scales = jnp.zeros((HEIGHT, half), jnp.float32)
        for start in range(0, HEIGHT, GROUP):
            col0 = base - lane0 + start
            spread = [
                jnp.broadcast_to(tiles[0][start:, col0 + j : col0 + j + 1], (HEIGHT - start, half))
                for j in range(GROUP)
            ]
            done = [t[:start] for t in tiles]
            live = [t[start:] for t in tiles]
            live_ids = ids[start:]
            for p in range(GROUP):
                pivot = spread[p][p : p + 1]
                scales = jnp.where(ids == start + p, lax.rsqrt(pivot), scales)
                ratio = jnp.where(live_ids > start + p, spread[p] * (1.0 / pivot), 0.0)
                for j in range(p + 1, GROUP):
                    spread[j] = spread[j] - ratio * spread[j][p : p + 1]
                live = [t - ratio * t[p : p + 1] for t in live]
            tiles = [
                jnp.concatenate([d, t], axis=0) if start else t for d, t in zip(done, live)
            ]
        tiles = [t * scales for t in tiles]
        for t in range(3):
            work[base : base + HEIGHT, lane0 + half * t : lane0 + half * (t + 1)] = tiles[t]
        after = base + HEIGHT
        if after < n:
            right = jnp.concatenate(tiles, axis=1)
            left = jnp.concatenate(tiles[:2], axis=1) if base < half else tiles[0]
            change = lax.dot_general(
                left, right, (((0,), (0,)), ((), ())), precision=HIGHEST,
                preferred_element_type=jnp.float32,
            )
            work[after:n, lane0 : lane0 + 3 * half] -= change[after - lane0 :]
    factor[...] = jnp.where(col_ids >= row_ids, work[:, 0:n], 0.0) * (1.0 / scale)
    inverse_high, inverse_low = two_parts(work[:, n : 2 * n] * scale)
    rows = image.shape[0]
    chunk = min(rows, 512)

    def solve(i, carry):
        here = pl.ds(pl.multiple_of(i * chunk, chunk), chunk)
        high, low = two_parts(image[here, :])
        solved = dot_turned(high, inverse_high) + dot_turned(high, inverse_low)
        basis[here, :] = (solved + dot_turned(low, inverse_high)).astype(basis.dtype)
        return carry

    lax.fori_loop(0, rows // chunk, solve, 0)


def factor_and_basis(gram, image, scale):
    rows, n = image.shape
    return pl.pallas_call(
        functools.partial(factor_kernel, scale),
        out_shape=(
            jax.ShapeDtypeStruct((rows, n), jnp.bfloat16),
            jax.ShapeDtypeStruct((n, n), jnp.float32),
        ),
        in_specs=[VMEM, VMEM],
        out_specs=(VMEM, VMEM),
        scratch_shapes=[pltpu.VMEM((n, 2 * n), jnp.float32)],
        compiler_params=pltpu.CompilerParams(vmem_limit_bytes=32 << 20),
        name="factor",
    )(gram, image)


def on_device(positions, sketch, counts, neighbours):
    blocks_z, blocks_y, _, points = positions.shape
    columns = sketch.shape[3]
    image, gram = image_and_gram(positions, sketch, counts, neighbours)
    total_rows = lax.axis_size("slab") * blocks_z * lax.axis_size("grp") * blocks_y * points
    basis, factor = factor_and_basis(gram, image, math.sqrt(total_rows))
    return basis.reshape(blocks_z, blocks_y, points, columns), factor


def solution(mesh):
    placed = (
        P("slab", "grp", None, None),
        P("slab", "grp", None, None),
        P("slab", "grp"),
        P("slab", "grp", None),
    )
    return jax.shard_map(
        on_device,
        mesh=mesh,
        in_specs=placed,
        out_specs=(P("slab", "grp", None, None), P()),
        check_vma=False,
    )
```
